32 devices in a mesh: pair: 8 (over y, x, core), virt: 4 (over z).
Axes of the slice: x: 2, y: 2, z: 4, core: 2. Of those that a mesh axis runs over, the one named last changes fastest.
Arguments:
- amps: bfloat16 [64, 1536, 1536], P('pair', 'virt'), may hold values from -6 to 6
- cycle_integrals: bfloat16 [1536, 1536], P('virt'), may hold values from -0.15625 to 0.15625
- mirror: int32 [64], replicated, may hold values from 0 to 63, as said below
- pair_list: int32 [64, 2], P('pair'), may hold values from 0 to 255, as said below
- tile_mask: int32 [64, 24], P('pair'), may hold values 0 or 1
- occ_energy: float32 [256], replicated, may hold values from -3 to -0.2
- virt_energy: float32 [1536], replicated, may hold values from 0.2 to 3
Outputs:
- update: bfloat16 [64, 1536, 1536], P('pair', 'virt')
The draws below stay inside these ranges and needn't reach their ends.
Inputs may be any that keep to these rules, and one draw needn't show every extreme that they name: `mirror`: a permutation of the 64 pair slots; slot p lies on index p // 8 of pair; the partners of the 8 slots of index d lie one each on the indices (d + 1 + k * 1) mod 8 for k = 0 to 7; which slot of d goes to which of these indices, and the position inside that index, are drawn. `pair_list`: each row holds i and j with i not larger than j.
All inputs are finite; a program needn't handle non-finite values. No bound on the sum of `tile_mask` on one device may be relied on, other than what follows from the above.
Results may differ from the reference program's by a relative error of at most 0.0049.
Values may be sent and summed in bfloat16 or wider, within the bound.
No kernel may reach another device: no remote copies, remote signals or barrier semaphores. Data moves between devices by JAX's collectives and lax.ppermute only.
A program may use at most 128 MiB of HBM per device.

```python
import jax
import jax.numpy as jnp
from jax import lax

V = 1536
NOCC = 256
TILE = 64
PAIR_DEV = 8
PAIRS = 64
NTILE = 24


def draw_mirror(key, part):
    key = jax.random.fold_in(key, 11)
    keys = jax.random.split(key, 2)
    devices = PAIRS // PAIR_DEV
    stride = devices // PAIR_DEV
    offsets = (1 + jnp.arange(PAIR_DEV, dtype=jnp.int32) * stride) % devices
    target = (jnp.arange(devices, dtype=jnp.int32)[:, None] + offsets[None, :]) % devices
    orders = jax.vmap(lambda k: jax.random.permutation(k, PAIR_DEV))(jax.random.split(keys[0], devices))
    sources = jax.vmap(lambda k: jax.random.permutation(k, PAIR_DEV))(jax.random.split(keys[1], devices))
    slot = orders[target, jnp.arange(PAIR_DEV)[None, :]]
    values = (target * PAIR_DEV + slot).reshape(-1).astype(jnp.int32)
    where_to = (jnp.arange(devices, dtype=jnp.int32)[:, None] * PAIR_DEV + sources).reshape(-1)
    return jnp.zeros((PAIRS,), jnp.int32).at[where_to].set(values).astype(jnp.int32)


def draw_pair_list(key, part):
    key = jax.random.fold_in(key, 17)
    keys = jax.random.split(key, 2)
    first = jax.random.randint(keys[0], (PAIRS,), 0, NOCC)
    second = jax.random.randint(keys[1], (PAIRS,), 0, NOCC)
    return jnp.stack([jnp.minimum(first, second), jnp.maximum(first, second)], axis=1).astype(jnp.int32)


def place_ends(drawn, rng, low, largest):
    extent = drawn.shape
    index_at = [jax.random.randint(jax.random.fold_in(rng, axis), (), 0, extent[axis]) for axis in range(len(extent))]
    drawn = drawn.at[tuple(index_at)].set(low)
    longest = extent.index(max(extent))
    index_at[longest] = (index_at[longest] + 1) % extent[longest]
    return drawn.at[tuple(index_at)].set(largest)


def steps_of(stream_key, extent, shards, smallest, top_value):
    factor_of = 1.0
    for dim, shards_of in shards:
        heights = jax.random.uniform(jax.random.fold_in(jax.random.fold_in(stream_key, 6), dim), (shards_of,), jnp.float32, smallest / len(shards), top_value / len(shards))
        factor_of = factor_of * jnp.repeat(jnp.exp(heights), extent[dim] // shards_of).reshape((-1,) + (1,) * (len(extent) - 1 - dim))
    return factor_of


def scatter_about(own_key, extent, deviation, bound, shards=(), kind=jnp.bfloat16):
    entries = jax.random.normal(own_key, extent, jnp.float32) * deviation
    if len(shards) > 0:
        entries = steps_of(own_key, extent, shards, -0.22, 0.18) * entries
    return jnp.clip(entries, min=-bound, max=bound).astype(kind)


def setup_inputs(seed: int = 0) -> dict:
    streams_of = jax.random.split(jax.random.key(seed), 8)
    return {
        "amps": scatter_about(streams_of[0], (PAIRS, V, V), 1.0, 6.0, ((0, 8), (1, 4))),
        "cycle_integrals": scatter_about(streams_of[1], (V, V), V ** -0.5, 0.15625, ((0, 4),)),
        "mirror": draw_mirror(jax.random.fold_in(streams_of[7], 71), 0),
        "pair_list": draw_pair_list(jax.random.fold_in(streams_of[7], 71), 0),
        "tile_mask": place_ends((jax.random.randint(streams_of[4], (PAIRS, NTILE), 0, 4) < 3).astype(jnp.int32), jax.random.fold_in(streams_of[4], 1), 0, 1),
        "occ_energy": jnp.clip(jax.random.uniform(streams_of[5], (NOCC,), jnp.float32, -3.0, -0.2), -3.0, -0.2),
        "virt_energy": jnp.clip(jax.random.uniform(streams_of[6], (V,), jnp.float32, 0.2, 3.0), 0.2, 3.0),
    }


def reference(amps, cycle_integrals, mirror, pair_list, tile_mask, occ_energy, virt_energy):
    def contract(block):
        return jnp.dot(block, cycle_integrals, preferred_element_type=jnp.float32).astype(jnp.bfloat16)

    contracted = lax.map(contract, amps)
    lanes = jnp.repeat(tile_mask, TILE, axis=1).astype(jnp.float32)
    occupied = occ_energy[pair_list[:, 0]] + occ_energy[pair_list[:, 1]]
    virt_sum = virt_energy[:, None] + virt_energy[None, :]

    def finish(index):
        own_block = contracted[index].astype(jnp.float32)
        partner = contracted[mirror[index]].astype(jnp.float32)
        cycle = 2.0 * own_block - partner
        denom = virt_sum - occupied[index]
        lane = lanes[index]
        return (cycle * lane[:, None] * lane[None, :] / denom).astype(jnp.bfloat16)

    return lax.map(finish, jnp.arange(PAIRS, dtype=jnp.int32))
```

```python
import functools

import jax
import jax.numpy as jnp
from jax import lax
from jax.experimental import pallas as pl
from jax.experimental.pallas import tpu as pltpu
from jax.sharding import PartitionSpec as P

TILE = 64
VMEM_BYTES = 24 * 1024 * 1024
FREE = pl.CostEstimate(flops=0, bytes_accessed=0, transcendentals=0)
ANY = pl.BlockSpec(memory_space=pl.ANY)
HBM = pl.BlockSpec(memory_space=pltpu.HBM)
WHOLE = pl.BlockSpec(memory_space=pltpu.VMEM)
SMEM = pl.BlockSpec(memory_space=pltpu.SMEM)


def in_hbm(array):
    return pltpu.with_memory_space_constraint(array, pltpu.HBM)


def in_vmem(array):
    return pltpu.with_memory_space_constraint(array, pltpu.VMEM)


def run_all(copies):
    for copy in copies:
        copy.start()
    for copy in copies:
        copy.wait()


def gate_kernel(*refs):
    del refs


def gate(values, earlier):
    count = len(values)
    return pl.pallas_call(
        gate_kernel,
        out_shape=[pltpu.HBM(value.shape, value.dtype) for value in values],
        in_specs=[ANY] * (count + len(earlier)),
        out_specs=[ANY] * count,
        input_output_aliases={n: n for n in range(count)},
        cost_estimate=FREE,
        name="gate",
    )(*[in_hbm(value) for value in values], *earlier)


def pick_kernel(parts, core_rows, *refs):
    slots_ref, amps_ref, shard_ref = refs[:3]
    outs, sems = refs[3:-1], refs[-1]
    copies = []
    for (steps, first, count), out in zip(parts, outs):
        for n, at in enumerate(steps):
            source = amps_ref.at[slots_ref[at], pl.ds(first, count)]
            copies.append(pltpu.make_async_copy(source, out.at[n], sems.at[len(copies)]))
    if core_rows:
        rows = pl.ds(slots_ref[slots_ref.shape[0] - 1] * core_rows, core_rows)
        copies.append(pltpu.make_async_copy(shard_ref.at[rows], outs[-1].at[0], sems.at[len(copies)]))
    run_all(copies)


def pick(parts, slots, amps, shard, core_rows=0, place=pltpu.VMEM):
    width = amps.shape[2]
    shapes = [place((len(steps), count, width), amps.dtype) for steps, _, count in parts]
    if core_rows:
        shapes.append(pltpu.HBM((1, core_rows, width), shard.dtype))
    return pl.pallas_call(
        functools.partial(pick_kernel, parts, core_rows),
        out_shape=shapes,
        in_specs=[SMEM, HBM, HBM],
        out_specs=[WHOLE] * len(shapes),
        scratch_shapes=[pltpu.SemaphoreType.DMA((sum(len(p[0]) for p in parts) + 1,))],
        compiler_params=pltpu.CompilerParams(vmem_limit_bytes=VMEM_BYTES),
        cost_estimate=FREE,
        name="pick",
    )(slots, in_hbm(amps), in_hbm(shard))


def assemble_kernel(crossing, count, place_ref, *refs):
    pieces, out_ref, sems = refs[:-2], refs[-2], refs[-1]
    z, core = place_ref[0], place_ref[1]
    copies = []
    for ref, first, mine in zip(pieces, *crossing):
        for n in range(ref.shape[0]):
            where = z ^ (first + n) if count == 4 else lax.rem(z + first + n, count)
            side = core if mine else 1 - core
            copies.append(pltpu.make_async_copy(ref.at[n], out_ref.at[where, side], sems.at[len(copies)]))
    run_all(copies)


def assemble(pieces, firsts, sides, place, count):
    _, half, width = pieces[0].shape
    full = pl.pallas_call(
        functools.partial(assemble_kernel, (firsts, sides), count),
        out_shape=pltpu.VMEM((count, 2, half, width), pieces[0].dtype),
        in_specs=[SMEM] + [ANY] * len(pieces),
        out_specs=WHOLE,
        scratch_shapes=[pltpu.SemaphoreType.DMA((2 * count,))],
        compiler_params=pltpu.CompilerParams(vmem_limit_bytes=VMEM_BYTES),
        cost_estimate=FREE,
        name="assemble",
    )(place, *map(in_hbm, pieces))
    return full.reshape(count * 2 * half, width)


def finish_kernel(whiches, owned, slots_ref, *refs):
    jobs = len(whiches)
    own_refs, refs = refs[:jobs if owned else 1], refs[jobs if owned else 1:]
    other_refs = refs[:jobs]
    k_ref, down_ref, across_ref = refs[jobs:jobs + 3]
    out_ref, mixed_ref = refs[-2:]
    step = pl.program_id(0)
    for job, (other_ref, which) in enumerate(zip(other_refs, whiches)):
        @pl.when(step == job)
        def _(job=job, other_ref=other_ref, which=which):
            own = own_refs[job if owned else 0][0]
            mixed_ref[...] = (own + own) - other_ref[which]

    cycle = jnp.dot(mixed_ref[...], k_ref[...], preferred_element_type=jnp.float32)
    denom = down_ref[0, :, 0:1] + across_ref[0, 0:1, :]
    kept = down_ref[0, :, 1:2] * across_ref[0, 1:2, :]
    out_ref[0] = (cycle * (kept / denom)).astype(out_ref.dtype)


def finish(first, jobs, slots, amps, integrals, down, across, so_far):
    pair_dev, _, width = amps.shape
    start, owns, others, whiches = zip(*jobs)
    owned = owns[0] is not None
    rows = others[0].shape[1]
    r = start[0] // rows
    own_specs = [WHOLE] * len(jobs) if owned else [pl.BlockSpec((1, rows, width), lambda n, s: (s[first + n], 0, 0))]
    in_specs = own_specs + [WHOLE] * (len(jobs) + 1) + [
        pl.BlockSpec((1, rows, 2), lambda n, s: (s[first + n], r, 0)),
        pl.BlockSpec((1, 2, width), lambda n, s: (s[first + n], 0, 0)),
    ]
    operands = [slots] + ([in_vmem(own) for own in owns] if owned else [in_hbm(amps)])
    operands += [in_vmem(other) if owned else other for other in others] + [in_vmem(integrals), down, across]
    aliases = {}
    if so_far is not None:
        aliases = {len(operands): 0}
        in_specs.append(ANY)
        operands.append(so_far)
    return pl.pallas_call(
        functools.partial(finish_kernel, whiches, owned),
        grid_spec=pltpu.PrefetchScalarGridSpec(
            num_scalar_prefetch=1,
            grid=(len(jobs),),
            in_specs=in_specs,
            out_specs=pl.BlockSpec((1, rows, width), lambda n, s: (s[first + n], r, 0)),
            scratch_shapes=[pltpu.VMEM((rows, width), jnp.bfloat16)],
        ),
        out_shape=jax.ShapeDtypeStruct(amps.shape, amps.dtype),
        input_output_aliases=aliases,
        compiler_params=pltpu.CompilerParams(vmem_limit_bytes=VMEM_BYTES),
        cost_estimate=FREE,
        name="finish",
    )(*operands)


def local(amps, cycle_integrals, mirror, pair_list, tile_mask, occ_energy, virt_energy):
    pair_dev, rows, width = amps.shape
    devices, planes = lax.axis_size("pair"), lax.axis_size("virt")
    here, column = lax.axis_index("pair"), lax.axis_index("virt")
    stride = devices // pair_dev
    crossing = stride == 1 and pair_dev == 8 and planes == 4
    order = [0, 1, 2, 4, 3, 5, 6, 7] if crossing else list(range(pair_dev))
    core = here % 2

    def move(block, axis, to):
        n = lax.axis_size(axis)
        return lax.ppermute(block, axis, [(i, to(i)) for i in range(n)])

    if crossing:
        target = source = here ^ jnp.array(order, dtype=jnp.int32)
    else:
        offsets = 1 + stride * jnp.arange(pair_dev, dtype=jnp.int32)
        target, source = (here - offsets) % devices, (here + offsets) % devices
    entries = mirror.reshape(devices, pair_dev)
    owner, inside = entries // pair_dev, entries % pair_dev
    place = jnp.arange(devices, dtype=jnp.int32)[None, :, None]
    slot = jnp.arange(pair_dev, dtype=jnp.int32)[None, None, :]
    target, source = target[:, None, None], source[:, None, None]
    outgoing = jnp.sum(jnp.where((place == target) & (owner[None] == here), inside[None], 0), axis=(1, 2))
    incoming = jnp.sum(jnp.where((place == here) & (owner[None] == source), slot, 0), axis=(1, 2))
    slots = jnp.concatenate([outgoing, incoming, core[None]]).astype(jnp.int32)

    def swap_cores(block):
        return move(block, "pair", lambda i: i ^ 1)

    core_rows = cycle_integrals.shape[0] // 2
    place = jnp.stack([column, core]).astype(jnp.int32)
    if crossing:
        cut = rows * 3 // 4
        out_at = {step: at for at, step in enumerate(order)}
        in_at = {step: pair_dev + at for at, step in enumerate(order)}
        to_x, to_y, to1, rows0 = pick(
            [((out_at[2], out_at[3]), 0, rows), ((out_at[4], out_at[5]), 0, rows), ((out_at[1],), 0, rows)],
            slots, amps, cycle_integrals, core_rows,
        )
        from_x = move(to_x, "pair", lambda i: i ^ 2)
        from_y = move(to_y, "pair", lambda i: i ^ 4)
        rows1, rows2 = move(rows0, "virt", lambda z: z ^ 1), move(rows0, "virt", lambda z: z ^ 2)
        rows3 = move(rows2, "virt", lambda z: z ^ 1)
        pieces = [rows0, rows1, rows2, rows3]
        pieces += [swap_cores(piece) for piece in pieces]
        integrals = assemble(pieces, [0, 1, 2, 3] * 2, [1] * 4 + [0] * 4, place, planes)
        from1 = swap_cores(to1)
        at6, at7 = (out_at[6],), (out_at[7],)
        in6, in7 = (in_at[6],), (in_at[7],)
        to0, to6, to7a, to7b = pick(
            [((out_at[0],), 0, rows), (at6, 0, rows), (at7, 0, cut), (at7, cut, rows - cut)],
            slots, amps, cycle_integrals, place=pltpu.HBM,
        )
        to6, to7a, to7b, from_x, from_y = gate([to6, to7a, to7b, from_x, from_y], [*pieces, from1])
        own6, own7a, own7b = pick(
            [(in6, 0, rows), (in7, 0, cut), (in7, cut, rows - cut)], slots, amps, cycle_integrals
        )
        from6, from7a, from7b = [move(block, "pair", lambda i, j=j: i ^ j) for j, block in ((6, to6), (7, to7a), (7, to7b))]
        swap_x, swap_y = swap_cores(from_x), swap_cores(from_y)
        calls = [
            [(0, None, to0, 0), (0, None, from1, 0), (0, None, from_x, 0), (0, None, from_y, 0)],
            [(0, None, swap_x, 1), (0, None, swap_y, 1)],
            [(0, own6, from6, 0)],
            [(0, own7a, from7a, 0)],
            [(cut, own7b, from7b, 0)],
        ]
        firsts = [in_at[0], in_at[3], in_at[6], in_at[7], in_at[7]]
    else:
        *to_all, rows0 = pick([((k,), 0, rows) for k in range(pair_dev)], slots, amps, cycle_integrals, core_rows)
        mine = [rows0] + [move(rows0, "virt", lambda z, s=s: (z - s) % planes) for s in range(1, planes)]
        other = [swap_cores(piece) for piece in mine]
        integrals = assemble(
            mine + other, 2 * list(range(planes)), [1] * planes + [0] * planes, place, planes
        )
        calls, firsts = [], []
        for k in range(pair_dev):
            arrived = move(to_all[k], "pair", lambda i, k=k: (i - 1 - k * stride) % devices)
            calls.append([(0, None, arrived, 0)])
            firsts.append(pair_dev + k)

    lanes = jnp.repeat(tile_mask, TILE, axis=1).astype(jnp.float32)
    lanes_rows = lax.dynamic_slice_in_dim(lanes, column * rows, rows, 1)
    energy_rows = lax.dynamic_slice_in_dim(virt_energy, column * rows, rows, 0)
    orbitals = jnp.arange(occ_energy.shape[0], dtype=jnp.int32)
    first = jnp.sum(jnp.where(pair_list[:, 0:1] == orbitals[None, :], occ_energy[None, :], 0.0), axis=1)
    second = jnp.sum(jnp.where(pair_list[:, 1:2] == orbitals[None, :], occ_energy[None, :], 0.0), axis=1)
    occupied = first + second
    down = jnp.stack([energy_rows[None, :] - occupied[:, None], lanes_rows], axis=-1)
    across = jnp.stack([jnp.broadcast_to(virt_energy[None, :], lanes.shape), lanes], axis=1)

    result = None
    for first_slot, jobs in zip(firsts, calls):
        result = finish(first_slot, jobs, slots, amps, integrals, down, across, result)
    return result


def solution(mesh):
    return jax.shard_map(
        local,
        mesh=mesh,
        in_specs=(
            P("pair", "virt", None),
            P("virt", None),
            P(),
            P("pair", None),
            P("pair", None),
            P(),
            P(),
        ),
        out_specs=P("pair", "virt", None),
        check_vma=False,
    )
```

```python
import functools

import jax
import jax.numpy as jnp
from jax import lax
from jax.experimental import pallas as pl
from jax.experimental.pallas import tpu as pltpu
from jax.sharding import PartitionSpec as P

TILE = 64
VMEM_BYTES = 16 * 1024 * 1024
PIECES = 3
FREE = pl.CostEstimate(flops=0, bytes_accessed=0, transcendentals=0)
ANY = pl.BlockSpec(memory_space=pl.ANY)
HBM = pl.BlockSpec(memory_space=pltpu.HBM)
WHOLE = pl.BlockSpec(memory_space=pltpu.VMEM)
SMEM = pl.BlockSpec(memory_space=pltpu.SMEM)


def in_hbm(array):
    return pltpu.with_memory_space_constraint(array, pltpu.HBM)


def in_vmem(array):
    return pltpu.with_memory_space_constraint(array, pltpu.VMEM)


def run_all(copies):
    for copy in copies:
        copy.start()
    for copy in copies:
        copy.wait()


def pick_kernel(picks, core_rows, pair_dev, waits, *refs):
    mirror_ref, amps_ref, shard_ref = refs[:3]
    outs, sems = refs[3 + waits:-1], refs[-1]
    here = lax.axis_index("pair")
    copies = []

    def slot_of(peer, outgoing):
        found = jnp.int32(0)
        for e in range(pair_dev):
            entry = mirror_ref[(peer if outgoing else here) * pair_dev + e]
            if pair_dev & (pair_dev - 1) == 0:
                owner = lax.shift_right_logical(entry, jnp.int32(pair_dev.bit_length() - 1))
                inside = entry & (pair_dev - 1)
            else:
                owner = lax.div(entry, jnp.int32(pair_dev))
                inside = lax.rem(entry, jnp.int32(pair_dev))
            value = inside if outgoing else jnp.int32(e)
            found = found + jnp.where(owner == (here if outgoing else peer), value, 0)
        return found

    for (parts, outgoing), out in zip(picks, outs):
        done = 0
        for peer, first, count in parts:
            slot = slot_of(peer(here), outgoing)
            for at in range(0, count, count // PIECES):
                size = count // PIECES
                source = amps_ref.at[slot, pl.ds(first + at, size)]
                copies.append(pltpu.make_async_copy(source, out.at[0, pl.ds(done + at, size)], sems.at[len(copies)]))
                copies[-1].start()
            done += count
    if core_rows:
        rows = pl.ds((here & 1) * core_rows, core_rows)
        copies.append(pltpu.make_async_copy(shard_ref.at[rows], outs[-1].at[0], sems.at[len(copies)]))
        copies[-1].start()
    for copy in copies:
        copy.wait()


def pick(picks, mirror, amps, shard, core_rows=0, place=pltpu.VMEM, earlier=()):
    pair_dev, _, width = amps.shape
    shapes = [place((1, sum(p[2] for p in parts), width), amps.dtype) for parts, _ in picks]
    if core_rows:
        shapes.append(place((1, core_rows, width), shard.dtype))
    return pl.pallas_call(
        functools.partial(pick_kernel, picks, core_rows, pair_dev, len(earlier)),
        out_shape=shapes,
        in_specs=[SMEM, HBM, HBM] + [ANY] * len(earlier),
        out_specs=[WHOLE] * len(shapes),
        scratch_shapes=[pltpu.SemaphoreType.DMA((PIECES * sum(len(parts) for parts, _ in picks) + 1,))],
        compiler_params=pltpu.CompilerParams(vmem_limit_bytes=VMEM_BYTES),
        cost_estimate=FREE,
        name="pick",
    )(mirror, in_hbm(amps), in_hbm(shard), *earlier)


def extract_kernel(parts, *refs):
    out_ref, sems = refs[-2:]
    copies, done = [], 0
    for n, (start, count) in enumerate(parts):
        source, target = refs[n].at[0, pl.ds(start, count)], out_ref.at[0, pl.ds(done, count)]
        copies.append(pltpu.make_async_copy(source, target, sems.at[n]))
        done += count
    run_all(copies)


def extract(parts, earlier=()):
    arrays = [array for array, _, _ in parts]
    rows, width = sum(count for _, _, count in parts), arrays[0].shape[2]
    return pl.pallas_call(
        functools.partial(extract_kernel, [part[1:] for part in parts]),
        out_shape=pltpu.VMEM((1, rows, width), arrays[0].dtype),
        in_specs=[ANY] * (len(arrays) + len(earlier)),
        out_specs=WHOLE,
        scratch_shapes=[pltpu.SemaphoreType.DMA((len(parts),))],
        compiler_params=pltpu.CompilerParams(vmem_limit_bytes=VMEM_BYTES),
        cost_estimate=FREE,
        name="extract",
    )(*arrays, *earlier)


def assemble_kernel(crossing, count, place_ref, *refs):
    pieces, out_ref, sems = refs[:-2], refs[-2], refs[-1]
    z, core = place_ref[0], place_ref[1]
    copies = []
    for ref, first, mine in zip(pieces, *crossing):
        for n in range(ref.shape[0]):
            where = z ^ (first + n) if count == 4 else lax.rem(z + first + n, count)
            side = core if mine else 1 - core
            copies.append(pltpu.make_async_copy(ref.at[n], out_ref.at[where, side], sems.at[len(copies)]))
    run_all(copies)


def assemble(pieces, firsts, sides, place, count):
    _, half, width = pieces[0].shape
    full = pl.pallas_call(
        functools.partial(assemble_kernel, (firsts, sides), count),
        out_shape=pltpu.VMEM((count, 2, half, width), pieces[0].dtype),
        in_specs=[SMEM] + [ANY] * len(pieces),
        out_specs=WHOLE,
        scratch_shapes=[pltpu.SemaphoreType.DMA((2 * count,))],
        compiler_params=pltpu.CompilerParams(vmem_limit_bytes=VMEM_BYTES),
        cost_estimate=FREE,
        name="assemble",
    )(place, *map(in_hbm, pieces))
    return full.reshape(count * 2 * half, width)


def finish_kernel(jobs, owned, slots_ref, *refs):
    own_ref, refs = refs[0], refs[1:]
    count = sum(map(len, jobs))
    other_refs, (k_ref, down_ref, across_ref) = list(refs[:count]), refs[count:count + 3]
    out_ref, token_ref, mixed_ref = refs[-3:]
    step = pl.program_id(0)
    token_ref[...] = jnp.zeros_like(token_ref)
    for job, lengths in enumerate(jobs):
        parts = [(other_refs.pop(0), length) for length in lengths]

        @pl.when(step == job)
        def _(parts=parts):
            first = 0
            for other_ref, length in parts:
                rows = pl.ds(first, length)
                own = own_ref[0, rows]
                mixed_ref[rows] = (own + own) - other_ref[0]
                first += length

    cycle = jnp.dot(mixed_ref[...], k_ref[...], preferred_element_type=jnp.float32)
    denom = down_ref[0, :, 0:1] + across_ref[0, 0:1, :]
    kept = down_ref[0, :, 1:2] * across_ref[0, 1:2, :]
    out_ref[0] = (cycle * (kept / denom)).astype(out_ref.dtype)


def finish(first, first_row, jobs, slots, amps, integrals, down, across, so_far, own=None):
    _, _, width = amps.shape
    rows = sum(length for _, _, length in jobs[0])
    r = first_row // rows
    others = [other for job in jobs for other, _, _ in job]
    in_specs = [pl.BlockSpec((1, rows, width), lambda n, s: (s[first + n], r, 0)) if own is None else WHOLE]
    for job in jobs:
        for _, start, length in job:
            in_specs.append(pl.BlockSpec((1, length, width), lambda n, s, at=start // length: (0, at, 0)))
    in_specs += [
        WHOLE,
        pl.BlockSpec((1, rows, 2), lambda n, s: (s[first + n], r, 0)),
        pl.BlockSpec((1, 2, width), lambda n, s: (s[first + n], 0, 0)),
    ]
    operands = [slots, in_hbm(amps) if own is None else in_vmem(own)]
    operands += others + [in_vmem(integrals), down, across]
    aliases = {}
    if so_far is not None:
        aliases = {len(operands): 0}
        in_specs.append(ANY)
        operands.append(so_far)
    return pl.pallas_call(
        functools.partial(finish_kernel, [[length for _, _, length in job] for job in jobs], own is not None),
        grid_spec=pltpu.PrefetchScalarGridSpec(
            num_scalar_prefetch=1,
            grid=(len(jobs),),
            in_specs=in_specs,
            out_specs=[
                pl.BlockSpec((1, rows, width), lambda n, s: (s[first + n], r, 0)),
                pl.BlockSpec((8, 128), lambda n, s: (0, 0)),
            ],
            scratch_shapes=[pltpu.VMEM((rows, width), jnp.bfloat16)],
        ),
        out_shape=[jax.ShapeDtypeStruct(amps.shape, amps.dtype), jax.ShapeDtypeStruct((8, 128), jnp.float32)],
        input_output_aliases=aliases,
        compiler_params=pltpu.CompilerParams(vmem_limit_bytes=VMEM_BYTES),
        cost_estimate=FREE,
        name="finish",
    )(*operands)


def finish_together_kernel(first, first_row, jobs, columns, slots_ref, *refs):
    count = len(jobs)
    rows = sum(length for _, length in jobs[0])
    own_refs, refs = refs[:count], refs[count:]
    parts = sum(map(len, jobs))
    other_refs, (k_ref, down_ref, across_ref) = list(refs[:parts]), refs[parts:parts + 3]
    out_ref, mixed_ref, done_ref, sems = refs[-4:]
    for job, lengths in enumerate(jobs):
        at = 0
        for start, length in lengths:
            other_ref = other_refs.pop(0)
            own = own_refs[job][0, pl.ds(at, length)]
            mixed_ref[pl.ds(job * rows + at, length)] = (own + own) - other_ref[0, pl.ds(start, length)]
            at += length
    copies = []
    for n in range(out_ref.shape[2] // columns):
        part = pl.ds(n * columns, columns)
        cycle = jnp.dot(mixed_ref[...], k_ref[:, part], preferred_element_type=jnp.float32)
        for job in range(count):
            slot = slots_ref[first + job]
            mine, here = pl.ds(job * rows, rows), pl.ds(first_row, rows)
            denom = down_ref[slot, here, 0:1] + across_ref[slot, 0:1, part]
            kept = down_ref[slot, here, 1:2] * across_ref[slot, 1:2, part]
            done_ref[mine, part] = (cycle[job * rows:(job + 1) * rows] * (kept / denom)).astype(done_ref.dtype)
            target = out_ref.at[slot, here, part]
            copies.append(pltpu.make_async_copy(done_ref.at[mine, part], target, sems.at[len(copies)]))
            copies[-1].start()
    for copy in copies:
        copy.wait()


def finish_together(first, first_row, jobs, slots, owns, integrals, down, across, so_far, columns=512):
    width = integrals.shape[1]
    rows = sum(length for _, _, length in jobs[0])
    others = [other for job in jobs for other, _, _ in job]
    steps = width // columns
    operands = [slots, *map(in_vmem, owns), *others, in_vmem(integrals), down, across, so_far]
    return pl.pallas_call(
        functools.partial(
            finish_together_kernel, first, first_row, [[part[1:] for part in job] for job in jobs], columns
        ),
        in_specs=[SMEM] + [WHOLE] * (len(operands) - 2) + [ANY],
        out_specs=ANY,
        out_shape=jax.ShapeDtypeStruct(so_far.shape, so_far.dtype),
        scratch_shapes=[
            pltpu.VMEM((len(jobs) * rows, width), jnp.bfloat16),
            pltpu.VMEM((len(jobs) * rows, width), jnp.bfloat16),
            pltpu.SemaphoreType.DMA((steps * len(jobs),)),
        ],
        input_output_aliases={len(operands) - 1: 0},
        compiler_params=pltpu.CompilerParams(vmem_limit_bytes=VMEM_BYTES),
        cost_estimate=FREE,
        name="finish_together",
    )(*operands)


def local(amps, cycle_integrals, mirror, pair_list, tile_mask, occ_energy, virt_energy):
    pair_dev, rows, width = amps.shape
    devices, planes = lax.axis_size("pair"), lax.axis_size("virt")
    here, column = lax.axis_index("pair"), lax.axis_index("virt")
    stride = devices // pair_dev
    crossing = stride == 1 and pair_dev == 8 and planes == 4
    order = [0, 1, 6, 7, 2, 4, 3, 5] if crossing else list(range(pair_dev))
    core = here % 2

    def move(block, axis, to):
        n = lax.axis_size(axis)
        return lax.ppermute(block, axis, [(i, to(i)) for i in range(n)])

    if crossing:
        source = here ^ jnp.array(order, dtype=jnp.int32)
    else:
        source = (here + 1 + stride * jnp.arange(pair_dev, dtype=jnp.int32)) % devices
    entries = lax.dynamic_slice_in_dim(mirror, here * pair_dev, pair_dev, 0)
    slot = jnp.arange(pair_dev, dtype=jnp.int32)
    slots = jnp.sum(jnp.where(entries[None, :] // pair_dev == source[:, None], slot[None, :], 0), axis=1)

    def swap_cores(block):
        return move(block, "pair", lambda i: i ^ 1)

    lanes = jnp.repeat(tile_mask, TILE, axis=1).astype(jnp.float32)
    lanes_rows = lax.dynamic_slice_in_dim(lanes, column * rows, rows, 1)
    energy_rows = lax.dynamic_slice_in_dim(virt_energy, column * rows, rows, 0)
    orbitals = jnp.arange(occ_energy.shape[0], dtype=jnp.int32)
    first = jnp.sum(jnp.where(pair_list[:, 0:1] == orbitals[None, :], occ_energy[None, :], 0.0), axis=1)
    second = jnp.sum(jnp.where(pair_list[:, 1:2] == orbitals[None, :], occ_energy[None, :], 0.0), axis=1)
    occupied = first + second
    down = jnp.stack([energy_rows[None, :] - occupied[:, None], lanes_rows], axis=-1)
    across = jnp.stack([jnp.broadcast_to(virt_energy[None, :], lanes.shape), lanes], axis=1)

    def run(first, first_row, jobs, integrals, so_far):
        return finish(first, first_row, jobs, slots, amps, integrals, down, across, so_far)

    core_rows = cycle_integrals.shape[0] // 2
    place = jnp.stack([column, core]).astype(jnp.int32)
    if crossing:
        in_at = {step: at for at, step in enumerate(order)}
        quarter = rows // 4

        def peer(step):
            return lambda i: i ^ step

        def take(parts, earlier=(), outgoing=True, core_rows=0, place=pltpu.VMEM):
            picks = [([(peer(step), first, count) for step, first, count in part], outgoing) for part in parts]
            return pick(picks, mirror, amps, cycle_integrals, core_rows, place, earlier)

        def shift(value, step):
            return move(value, "pair", peer(step))

        def whole(step):
            return (step, 0, rows)

        def quarters(step, first, count):
            return (step, first * quarter, count * quarter)

        to_d, to1, rows0 = take([[whole(6), whole(7)], [whole(1)]], core_rows=core_rows)
        from_d, from1 = shift(to_d, 6), swap_cores(to1)
        rows1, rows2 = move(rows0, "virt", lambda z: z ^ 1), move(rows0, "virt", lambda z: z ^ 2)
        rows3 = move(rows2, "virt", lambda z: z ^ 1)
        pieces = [rows0, rows1, rows2, rows3]
        pieces += [swap_cores(piece) for piece in pieces]
        integrals = assemble(pieces, [0, 1, 2, 3] * 2, [1] * 4 + [0] * 4, place, planes)
        to_x, to_y = take(
            [[whole(2), quarters(3, 0, 1)], [whole(4), quarters(5, 0, 1)]], [rows1, rows2, slots, down, across]
        )
        from_x, from_y = shift(to_x, 2), shift(to_y, 4)
        to0, = take([[whole(0)]], [rows1])
        tails = take([[quarters(3, 1, 2)], [quarters(5, 1, 2)]], [from_d])
        from3, from5 = shift(tails[0], 3), shift(tails[1], 5)
        swap_d = swap_cores(extract([(from_d, rows, rows)]))
        parts = [[(part, 0, rows)] for part in (to0, from1, from_d, swap_d)]
        result, done = run(0, 0, parts, integrals, None)
        last = take([[quarters(3, 3, 1)], [quarters(5, 3, 1)]], [from_d])
        owns = take([[whole(2)], [whole(4)]], [from_d], False)
        owns += take([[quarters(s, *q)] for q in ((0, 3), (3, 1)) for s in (3, 5)], [from_d], False)
        swapped = swap_cores(extract([(from_x, rows, quarter), (from_y, rows, quarter)], [done, *last, *owns]))
        last3, last5 = shift(last[0], 3), shift(last[1], 5)

        def together(first, first_row, parts, owns, so_far):
            return finish_together(first, first_row, parts, slots, owns, integrals, down, across, so_far)

        parts = [[(from_x, 0, rows)], [(from_y, 0, rows)]]
        result = together(in_at[2], 0, parts, owns[:2], result)
        parts = [[(swapped, n * quarter, quarter), (direct, 0, 2 * quarter)] for n, direct in enumerate((from3, from5))]
        result = together(in_at[3], 0, parts, owns[2:4], result)
        parts = [[(last3, 0, quarter)], [(last5, 0, quarter)]]
        result = together(in_at[3], 3 * quarter, parts, owns[4:], result)
    else:
        picks = []
        for k in range(pair_dev):
            offset = (1 + k * stride) % devices
            picks.append(([(lambda i, o=offset: lax.rem(i + devices - o, jnp.int32(devices)), 0, rows)], True))
        *to_all, rows0 = pick(picks, mirror, amps, cycle_integrals, core_rows, pltpu.HBM)
        mine = [rows0] + [move(rows0, "virt", lambda z, s=s: (z - s) % planes) for s in range(1, planes)]
        other = [swap_cores(piece) for piece in mine]
        integrals = assemble(
            mine + other, 2 * list(range(planes)), [1] * planes + [0] * planes, place, planes
        )
        result = None
        for k in range(pair_dev):
            arrived = move(to_all[k], "pair", lambda i, k=k: (i - 1 - k * stride) % devices)
            result, _ = run(k, 0, [[(arrived, 0, rows)]], integrals, result)
    return result


def solution(mesh):
    return jax.shard_map(
        local,
        mesh=mesh,
        in_specs=(
            P("pair", "virt", None),
            P("virt", None),
            P(),
            P("pair", None),
            P("pair", None),
            P(),
            P(),
        ),
        out_specs=P("pair", "virt", None),
        check_vma=False,
    )
```

```python
import functools

import jax
import jax.numpy as jnp
from jax import lax
from jax.experimental import pallas as pl
from jax.experimental.pallas import tpu as pltpu
from jax.sharding import PartitionSpec as P

TILE = 64
VMEM_BYTES = 16 * 1024 * 1024
PIECES = 3
FREE = pl.CostEstimate(flops=0, bytes_accessed=0, transcendentals=0)
ANY = pl.BlockSpec(memory_space=pl.ANY)
HBM = pl.BlockSpec(memory_space=pltpu.HBM)
WHOLE = pl.BlockSpec(memory_space=pltpu.VMEM)
SMEM = pl.BlockSpec(memory_space=pltpu.SMEM)


def in_hbm(array):
    return pltpu.with_memory_space_constraint(array, pltpu.HBM)


def in_vmem(array):
    return pltpu.with_memory_space_constraint(array, pltpu.VMEM)


def run_all(copies):
    for copy in copies:
        copy.start()
    for copy in copies:
        copy.wait()


def pick_kernel(picks, core_rows, pair_dev, waits, staged, *refs):
    mirror_ref, amps_ref, shard_ref = refs[:3]
    total = len(picks) + (core_rows > 0)
    outs, stages = refs[3 + waits:3 + waits + total], refs[3 + waits + total:-2] if staged else None
    sems, store_sems = refs[-2:]
    here = lax.axis_index("pair")

    def fetch(item, n):
        source, out, part = item
        return pltpu.make_async_copy(source, (stages if staged else outs)[out].at[0, part], sems.at[n])

    def store(item, n):
        _, out, part = item
        return pltpu.make_async_copy(stages[out].at[0, part], outs[out].at[0, part], store_sems.at[n])

    def slot_of(peer, outgoing):
        found = jnp.int32(0)
        for e in range(pair_dev):
            entry = mirror_ref[(peer if outgoing else here) * pair_dev + e]
            if pair_dev & (pair_dev - 1) == 0:
                owner = lax.shift_right_logical(entry, jnp.int32(pair_dev.bit_length() - 1))
                inside = entry & (pair_dev - 1)
            else:
                owner = lax.div(entry, jnp.int32(pair_dev))
                inside = lax.rem(entry, jnp.int32(pair_dev))
            value = inside if outgoing else jnp.int32(e)
            found = found + jnp.where(owner == (here if outgoing else peer), value, 0)
        return found

    moves = []
    for n, ((parts, outgoing), out) in enumerate(zip(picks, outs)):
        done = 0
        for peer, first, count in parts:
            slot = slot_of(peer(here), outgoing)
            size = count // PIECES if count % (16 * PIECES) == 0 else count
            for at in range(0, count, size):
                part = pl.ds(done + at, size)
                moves.append((amps_ref.at[slot, pl.ds(first + at, size)], n, part))
                fetch(moves[-1], len(moves) - 1).start()
            done += count
    if core_rows:
        rows = pl.ds(pl.multiple_of((here & 1) * core_rows, core_rows), core_rows)
        moves.append((shard_ref.at[rows], len(outs) - 1, pl.ds(0, core_rows)))
        fetch(moves[-1], len(moves) - 1).start()
    for n, item in enumerate(moves):
        fetch(item, n).wait()
        if staged:
            store(item, n).start()
    if staged:
        for n, item in enumerate(moves):
            store(item, n).wait()


def pick(picks, mirror, amps, shard, core_rows=0, earlier=(), staged=False):
    pair_dev, _, width = amps.shape
    shapes = [jax.ShapeDtypeStruct((1, sum(p[2] for p in parts), width), amps.dtype) for parts, _ in picks]
    if core_rows:
        shapes.append(jax.ShapeDtypeStruct((1, core_rows, width), shard.dtype))
    return pl.pallas_call(
        functools.partial(pick_kernel, picks, core_rows, pair_dev, len(earlier), staged),
        out_shape=shapes,
        in_specs=[SMEM, HBM, HBM] + [ANY] * len(earlier),
        out_specs=[ANY if staged else WHOLE] * len(shapes),
        scratch_shapes=([pltpu.VMEM(shape.shape, shape.dtype) for shape in shapes] if staged else [])
        + [pltpu.SemaphoreType.DMA((PIECES * sum(len(parts) for parts, _ in picks) + 1,))] * 2,
        compiler_params=pltpu.CompilerParams(vmem_limit_bytes=VMEM_BYTES),
        cost_estimate=FREE,
        name="pick",
    )(mirror, in_hbm(amps), in_hbm(shard), *earlier)


def extract_kernel(parts, *refs):
    out_ref, sems = refs[-2:]
    copies, done = [], 0
    for n, (start, count) in enumerate(parts):
        source, target = refs[n].at[0, pl.ds(start, count)], out_ref.at[0, pl.ds(done, count)]
        copies.append(pltpu.make_async_copy(source, target, sems.at[n]))
        done += count
    run_all(copies)


def extract(parts, earlier=()):
    arrays = [array for array, _, _ in parts]
    rows, width = sum(count for _, _, count in parts), arrays[0].shape[2]
    return pl.pallas_call(
        functools.partial(extract_kernel, [part[1:] for part in parts]),
        out_shape=pltpu.VMEM((1, rows, width), arrays[0].dtype),
        in_specs=[ANY] * (len(arrays) + len(earlier)),
        out_specs=WHOLE,
        scratch_shapes=[pltpu.SemaphoreType.DMA((len(parts),))],
        compiler_params=pltpu.CompilerParams(vmem_limit_bytes=VMEM_BYTES),
        cost_estimate=FREE,
        name="extract",
    )(*arrays, *earlier)


def assemble_kernel(crossing, count, place_ref, *refs):
    pieces, out_ref, sems = refs[:-2], refs[-2], refs[-1]
    z, core = place_ref[0], place_ref[1]
    copies = []
    for ref, first, mine in zip(pieces, *crossing):
        for n in range(ref.shape[0]):
            where = z ^ (first + n) if count == 4 else lax.rem(z + first + n, count)
            side = core if mine else 1 - core
            copies.append(pltpu.make_async_copy(ref.at[n], out_ref.at[where, side], sems.at[len(copies)]))
    run_all(copies)


def assemble(pieces, firsts, sides, place, count):
    _, half, width = pieces[0].shape
    full = pl.pallas_call(
        functools.partial(assemble_kernel, (firsts, sides), count),
        out_shape=pltpu.VMEM((count, 2, half, width), pieces[0].dtype),
        in_specs=[SMEM] + [ANY] * len(pieces),
        out_specs=WHOLE,
        scratch_shapes=[pltpu.SemaphoreType.DMA((2 * count,))],
        compiler_params=pltpu.CompilerParams(vmem_limit_bytes=VMEM_BYTES),
        cost_estimate=FREE,
        name="assemble",
    )(place, *map(in_hbm, pieces))
    return full.reshape(count * 2 * half, width)


def finish_kernel(jobs, owned, slots_ref, *refs):
    own_ref, refs = refs[0], refs[1:]
    count = sum(map(len, jobs))
    other_refs, (k_ref, down_ref, across_ref) = list(refs[:count]), refs[count:count + 3]
    out_ref, token_ref, mixed_ref = refs[-3:]
    step = pl.program_id(0)
    token_ref[...] = jnp.zeros_like(token_ref)
    for job, lengths in enumerate(jobs):
        parts = [(other_refs.pop(0), length) for length in lengths]

        @pl.when(step == job)
        def _(parts=parts):
            first = 0
            for other_ref, length in parts:
                rows = pl.ds(first, length)
                own = own_ref[0, rows]
                mixed_ref[rows] = (own + own) - other_ref[0]
                first += length

    cycle = jnp.dot(mixed_ref[...], k_ref[...], preferred_element_type=jnp.float32)
    denom = down_ref[0, :, 0:1] + across_ref[0, 0:1, :]
    kept = down_ref[0, :, 1:2] * across_ref[0, 1:2, :]
    out_ref[0] = (cycle * (kept / denom)).astype(out_ref.dtype)


def finish(first, first_row, jobs, slots, amps, integrals, down, across, so_far, own=None):
    _, _, width = amps.shape
    rows = sum(length for _, _, length in jobs[0])
    r = first_row // rows
    others = [other for job in jobs for other, _, _ in job]
    in_specs = [pl.BlockSpec((1, rows, width), lambda n, s: (s[first + n], r, 0)) if own is None else WHOLE]
    for job in jobs:
        for _, start, length in job:
            in_specs.append(pl.BlockSpec((1, length, width), lambda n, s, at=start // length: (0, at, 0)))
    in_specs += [
        WHOLE,
        pl.BlockSpec((1, rows, 2), lambda n, s: (s[first + n], r, 0)),
        pl.BlockSpec((1, 2, width), lambda n, s: (s[first + n], 0, 0)),
    ]
    operands = [slots, in_hbm(amps) if own is None else in_vmem(own)]
    operands += others + [in_vmem(integrals), down, across]
    aliases = {}
    if so_far is not None:
        aliases = {len(operands): 0}
        in_specs.append(ANY)
        operands.append(so_far)
    return pl.pallas_call(
        functools.partial(finish_kernel, [[length for _, _, length in job] for job in jobs], own is not None),
        grid_spec=pltpu.PrefetchScalarGridSpec(
            num_scalar_prefetch=1,
            grid=(len(jobs),),
            in_specs=in_specs,
            out_specs=[
                pl.BlockSpec((1, rows, width), lambda n, s: (s[first + n], r, 0)),
                pl.BlockSpec((8, 128), lambda n, s: (0, 0)),
            ],
            scratch_shapes=[pltpu.VMEM((rows, width), jnp.bfloat16)],
        ),
        out_shape=[jax.ShapeDtypeStruct(amps.shape, amps.dtype), jax.ShapeDtypeStruct((8, 128), jnp.float32)],
        input_output_aliases=aliases,
        compiler_params=pltpu.CompilerParams(vmem_limit_bytes=VMEM_BYTES),
        cost_estimate=FREE,
        name="finish",
    )(*operands)


def finish_together_kernel(first, first_row, jobs, columns, slots_ref, *refs):
    count = len(jobs)
    rows = sum(length for _, length in jobs[0])
    own_refs, refs = refs[:count], refs[count:]
    parts = sum(map(len, jobs))
    other_refs, (k_ref, down_ref, across_ref) = list(refs[:parts]), refs[parts:parts + 3]
    out_ref, mixed_ref, done_ref, sems = refs[-4:]
    for job, lengths in enumerate(jobs):
        at = 0
        for start, length in lengths:
            other_ref = other_refs.pop(0)
            own = own_refs[job][0, pl.ds(at, length)]
            mixed_ref[pl.ds(job * rows + at, length)] = (own + own) - other_ref[0, pl.ds(start, length)]
            at += length
    copies = []
    for n in range(out_ref.shape[2] // columns):
        part = pl.ds(n * columns, columns)
        cycle = jnp.dot(mixed_ref[...], k_ref[:, part], preferred_element_type=jnp.float32)
        for job in range(count):
            slot = slots_ref[first + job]
            mine, here = pl.ds(job * rows, rows), pl.ds(first_row, rows)
            denom = down_ref[slot, here, 0:1] + across_ref[slot, 0:1, part]
            kept = down_ref[slot, here, 1:2] * across_ref[slot, 1:2, part]
            done_ref[mine, part] = (cycle[job * rows:(job + 1) * rows] * (kept / denom)).astype(done_ref.dtype)
            target = out_ref.at[slot, here, part]
            copies.append(pltpu.make_async_copy(done_ref.at[mine, part], target, sems.at[len(copies)]))
            copies[-1].start()
    for copy in copies:
        copy.wait()


def finish_together(first, first_row, jobs, slots, owns, integrals, down, across, so_far, columns=512):
    width = integrals.shape[1]
    rows = sum(length for _, _, length in jobs[0])
    others = [other for job in jobs for other, _, _ in job]
    steps = width // columns
    operands = [slots, *map(in_vmem, owns), *others, in_vmem(integrals), down, across, so_far]
    return pl.pallas_call(
        functools.partial(
            finish_together_kernel, first, first_row, [[part[1:] for part in job] for job in jobs], columns
        ),
        in_specs=[SMEM] + [WHOLE] * (len(operands) - 2) + [ANY],
        out_specs=ANY,
        out_shape=jax.ShapeDtypeStruct(so_far.shape, so_far.dtype),
        scratch_shapes=[
            pltpu.VMEM((len(jobs) * rows, width), jnp.bfloat16),
            pltpu.VMEM((len(jobs) * rows, width), jnp.bfloat16),
            pltpu.SemaphoreType.DMA((steps * len(jobs),)),
        ],
        input_output_aliases={len(operands) - 1: 0},
        compiler_params=pltpu.CompilerParams(vmem_limit_bytes=VMEM_BYTES),
        cost_estimate=FREE,
        name="finish_together",
    )(*operands)


def local(amps, cycle_integrals, mirror, pair_list, tile_mask, occ_energy, virt_energy):
    pair_dev, rows, width = amps.shape
    devices, planes = lax.axis_size("pair"), lax.axis_size("virt")
    here, column = lax.axis_index("pair"), lax.axis_index("virt")
    stride = devices // pair_dev
    crossing = stride == 1 and pair_dev == 8 and planes == 4
    order = [0, 1, 6, 7, 2, 4, 3, 5] if crossing else list(range(pair_dev))
    core = here % 2

    def move(block, axis, to):
        n = lax.axis_size(axis)
        return lax.ppermute(block, axis, [(i, to(i)) for i in range(n)])

    if crossing:
        source = here ^ jnp.array(order, dtype=jnp.int32)
    else:
        source = (here + 1 + stride * jnp.arange(pair_dev, dtype=jnp.int32)) % devices
    entries = lax.dynamic_slice_in_dim(mirror, here * pair_dev, pair_dev, 0)
    slot = jnp.arange(pair_dev, dtype=jnp.int32)
    slots = jnp.sum(jnp.where(entries[None, :] // pair_dev == source[:, None], slot[None, :], 0), axis=1)

    def swap_cores(block):
        return move(block, "pair", lambda i: i ^ 1)

    lanes = jnp.repeat(tile_mask, TILE, axis=1).astype(jnp.float32)
    lanes_rows = lax.dynamic_slice_in_dim(lanes, column * rows, rows, 1)
    energy_rows = lax.dynamic_slice_in_dim(virt_energy, column * rows, rows, 0)
    orbitals = jnp.arange(occ_energy.shape[0], dtype=jnp.int32)
    first = jnp.sum(jnp.where(pair_list[:, 0:1] == orbitals[None, :], occ_energy[None, :], 0.0), axis=1)
    second = jnp.sum(jnp.where(pair_list[:, 1:2] == orbitals[None, :], occ_energy[None, :], 0.0), axis=1)
    occupied = first + second
    down = jnp.stack([energy_rows[None, :] - occupied[:, None], lanes_rows], axis=-1)
    across = jnp.stack([jnp.broadcast_to(virt_energy[None, :], lanes.shape), lanes], axis=1)

    def run(first, first_row, jobs, integrals, so_far):
        return finish(first, first_row, jobs, slots, amps, integrals, down, across, so_far)

    core_rows = cycle_integrals.shape[0] // 2
    place = jnp.stack([column, core]).astype(jnp.int32)
    if crossing:
        in_at = {step: at for at, step in enumerate(order)}
        quarter = rows // 4

        def peer(step):
            return lambda i: i ^ step

        def take(parts, earlier=(), outgoing=True, core_rows=0, staged=False):
            picks = [([(peer(step), first, count) for step, first, count in part], outgoing) for part in parts]
            return pick(picks, mirror, amps, cycle_integrals, core_rows, earlier, staged)

        def shift(value, step):
            return move(value, "pair", peer(step))

        def whole(step):
            return (step, 0, rows)

        def quarters(step, first, count):
            return (step, first * quarter, count * quarter)

        to_d, = take([[whole(6), whole(7)]], staged=True)
        to1, rows0 = take([[whole(1)]], [to_d], core_rows=core_rows, staged=True)
        from_d, from1 = shift(to_d, 6), swap_cores(to1)
        rows1, rows2 = move(rows0, "virt", lambda z: z ^ 1), move(rows0, "virt", lambda z: z ^ 2)
        rows3 = move(rows2, "virt", lambda z: z ^ 1)
        pieces = [rows0, rows1, rows2, rows3]
        pieces += [swap_cores(piece) for piece in pieces]
        integrals = assemble(pieces, [0, 1, 2, 3] * 2, [1] * 4 + [0] * 4, place, planes)
        to_x, to_y = take(
            [[whole(2), quarters(3, 0, 1)], [whole(4), quarters(5, 0, 1)]], [rows1, rows2, slots, down, across], staged=True
        )
        from_x, from_y = shift(to_x, 2), shift(to_y, 4)
        to0, = take([[whole(0)]], [rows1])
        tails = take([[quarters(3, 1, 2)], [quarters(5, 1, 2)]], [from_d])
        from3, from5 = shift(tails[0], 3), shift(tails[1], 5)
        swap_d = swap_cores(extract([(from_d, rows, rows)]))
        parts = [[(part, 0, rows)] for part in (to0, from1, from_d, swap_d)]
        result, done = run(0, 0, parts, integrals, None)
        last = take([[quarters(3, 3, 1)], [quarters(5, 3, 1)]], [from_d])
        owns = take([[whole(2)], [whole(4)]], [from_d], False)
        owns += take([[quarters(s, *q)] for q in ((0, 3), (3, 1)) for s in (3, 5)], [from_d], False)
        swapped = swap_cores(extract([(from_x, rows, quarter), (from_y, rows, quarter)], [done, *last, *owns]))
        last3, last5 = shift(last[0], 3), shift(last[1], 5)

        def together(first, first_row, parts, owns, so_far):
            return finish_together(first, first_row, parts, slots, owns, integrals, down, across, so_far)

        parts = [[(from_x, 0, rows)], [(from_y, 0, rows)]]
        result = together(in_at[2], 0, parts, owns[:2], result)
        parts = [[(swapped, n * quarter, quarter), (direct, 0, 2 * quarter)] for n, direct in enumerate((from3, from5))]
        result = together(in_at[3], 0, parts, owns[2:4], result)
        parts = [[(last3, 0, quarter)], [(last5, 0, quarter)]]
        result = together(in_at[3], 3 * quarter, parts, owns[4:], result)
    else:
        picks = []
        for k in range(pair_dev):
            offset = (1 + k * stride) % devices
            picks.append(([(lambda i, o=offset: lax.rem(i + devices - o, jnp.int32(devices)), 0, rows)], True))
        *to_all, rows0 = pick(picks, mirror, amps, cycle_integrals, core_rows)
        mine = [rows0] + [move(rows0, "virt", lambda z, s=s: (z - s) % planes) for s in range(1, planes)]
        other = [swap_cores(piece) for piece in mine]
        integrals = assemble(
            mine + other, 2 * list(range(planes)), [1] * planes + [0] * planes, place, planes
        )
        result = None
        for k in range(pair_dev):
            arrived = move(to_all[k], "pair", lambda i, k=k: (i - 1 - k * stride) % devices)
            result, _ = run(k, 0, [[(arrived, 0, rows)]], integrals, result)
    return result


def solution(mesh):
    return jax.shard_map(
        local,
        mesh=mesh,
        in_specs=(
            P("pair", "virt", None),
            P("virt", None),
            P(),
            P("pair", None),
            P("pair", None),
            P(),
            P(),
        ),
        out_specs=P("pair", "virt", None),
        check_vma=False,
    )
```

```python
import functools

import jax
import jax.numpy as jnp
from jax import lax
from jax.experimental import pallas as pl
from jax.experimental.pallas import tpu as pltpu
from jax.sharding import PartitionSpec as P

TILE = 64
VMEM_BYTES = 16 * 1024 * 1024
PIECES = 3
FREE = pl.CostEstimate(flops=0, bytes_accessed=0, transcendentals=0)
ANY = pl.BlockSpec(memory_space=pl.ANY)
HBM = pl.BlockSpec(memory_space=pltpu.HBM)
WHOLE = pl.BlockSpec(memory_space=pltpu.VMEM)
SMEM = pl.BlockSpec(memory_space=pltpu.SMEM)


def in_hbm(array):
    return pltpu.with_memory_space_constraint(array, pltpu.HBM)


def in_vmem(array):
    return pltpu.with_memory_space_constraint(array, pltpu.VMEM)


def run_all(copies):
    for copy in copies:
        copy.start()
    for copy in copies:
        copy.wait()


def pick_kernel(picks, core_rows, pair_dev, waits, staged, *refs):
    mirror_ref, amps_ref, shard_ref = refs[:3]
    if staged:
        refs, (own_mirror_ref, mirror_sem) = refs[:-2], refs[-2:]
        whole = pltpu.make_async_copy(mirror_ref, own_mirror_ref, mirror_sem)
        whole.start()
        whole.wait()
        mirror_ref = own_mirror_ref
    total = len(picks) + (core_rows > 0)
    outs, stages = refs[3 + waits:3 + waits + total], refs[3 + waits + total:-2] if staged else None
    sems, store_sems = refs[-2:]
    here = lax.axis_index("pair")

    def fetch(item, n):
        source, out, part = item
        return pltpu.make_async_copy(source, (stages if staged else outs)[out].at[0, part], sems.at[n])

    def store(item, n):
        _, out, part = item
        return pltpu.make_async_copy(stages[out].at[0, part], outs[out].at[0, part], store_sems.at[n])

    def slot_of(peer, outgoing):
        found = jnp.int32(0)
        for e in range(pair_dev):
            entry = mirror_ref[(peer if outgoing else here) * pair_dev + e]
            if pair_dev & (pair_dev - 1) == 0:
                owner = lax.shift_right_logical(entry, jnp.int32(pair_dev.bit_length() - 1))
                inside = entry & (pair_dev - 1)
            else:
                owner = lax.div(entry, jnp.int32(pair_dev))
                inside = lax.rem(entry, jnp.int32(pair_dev))
            value = inside if outgoing else jnp.int32(e)
            found = found + jnp.where(owner == (here if outgoing else peer), value, 0)
        return found

    moves = []
    for n, ((parts, outgoing), out) in enumerate(zip(picks, outs)):
        done = 0
        for peer, first, count in parts:
            slot = slot_of(peer(here), outgoing)
            size = count // PIECES if count % (16 * PIECES) == 0 else count
            for at in range(0, count, size):
                part = pl.ds(done + at, size)
                moves.append((amps_ref.at[slot, pl.ds(first + at, size)], n, part))
                fetch(moves[-1], len(moves) - 1).start()
            done += count
    if core_rows:
        rows = pl.ds(pl.multiple_of((here & 1) * core_rows, core_rows), core_rows)
        moves.append((shard_ref.at[rows], len(outs) - 1, pl.ds(0, core_rows)))
        fetch(moves[-1], len(moves) - 1).start()
    for n, item in enumerate(moves):
        fetch(item, n).wait()
        if staged:
            store(item, n).start()
    if staged:
        for n, item in enumerate(moves):
            store(item, n).wait()


def pick(picks, mirror, amps, shard, core_rows=0, earlier=(), staged=False):
    pair_dev, _, width = amps.shape
    shapes = [jax.ShapeDtypeStruct((1, sum(p[2] for p in parts), width), amps.dtype) for parts, _ in picks]
    if core_rows:
        shapes.append(jax.ShapeDtypeStruct((1, core_rows, width), shard.dtype))
    return pl.pallas_call(
        functools.partial(pick_kernel, picks, core_rows, pair_dev, len(earlier), staged),
        out_shape=shapes,
        in_specs=[HBM if staged else SMEM, HBM, HBM] + [ANY] * len(earlier),
        out_specs=[ANY if staged else WHOLE] * len(shapes),
        scratch_shapes=([pltpu.VMEM(shape.shape, shape.dtype) for shape in shapes] if staged else [])
        + [pltpu.SemaphoreType.DMA((PIECES * sum(len(parts) for parts, _ in picks) + 1,))] * 2
        + ([pltpu.SMEM(mirror.shape, mirror.dtype), pltpu.SemaphoreType.DMA] if staged else []),
        compiler_params=pltpu.CompilerParams(vmem_limit_bytes=VMEM_BYTES),
        cost_estimate=FREE,
        name="pick",
    )(in_hbm(mirror) if staged else mirror, in_hbm(amps), in_hbm(shard), *earlier)


def extract_kernel(parts, *refs):
    out_ref, sems = refs[-2:]
    copies, done = [], 0
    for n, (start, count) in enumerate(parts):
        source, target = refs[n].at[0, pl.ds(start, count)], out_ref.at[0, pl.ds(done, count)]
        copies.append(pltpu.make_async_copy(source, target, sems.at[n]))
        done += count
    run_all(copies)


def extract(parts, earlier=()):
    arrays = [array for array, _, _ in parts]
    rows, width = sum(count for _, _, count in parts), arrays[0].shape[2]
    return pl.pallas_call(
        functools.partial(extract_kernel, [part[1:] for part in parts]),
        out_shape=pltpu.VMEM((1, rows, width), arrays[0].dtype),
        in_specs=[ANY] * (len(arrays) + len(earlier)),
        out_specs=WHOLE,
        scratch_shapes=[pltpu.SemaphoreType.DMA((len(parts),))],
        compiler_params=pltpu.CompilerParams(vmem_limit_bytes=VMEM_BYTES),
        cost_estimate=FREE,
        name="extract",
    )(*arrays, *earlier)


def assemble_kernel(crossing, count, place_ref, *refs):
    pieces, out_ref, sems = refs[:-2], refs[-2], refs[-1]
    z, core = place_ref[0], place_ref[1]
    copies = []
    for ref, first, mine in zip(pieces, *crossing):
        for n in range(ref.shape[0]):
            where = z ^ (first + n) if count == 4 else lax.rem(z + first + n, count)
            side = core if mine else 1 - core
            copies.append(pltpu.make_async_copy(ref.at[n], out_ref.at[where, side], sems.at[len(copies)]))
    run_all(copies)


def assemble(pieces, firsts, sides, place, count):
    _, half, width = pieces[0].shape
    full = pl.pallas_call(
        functools.partial(assemble_kernel, (firsts, sides), count),
        out_shape=pltpu.VMEM((count, 2, half, width), pieces[0].dtype),
        in_specs=[SMEM] + [ANY] * len(pieces),
        out_specs=WHOLE,
        scratch_shapes=[pltpu.SemaphoreType.DMA((2 * count,))],
        compiler_params=pltpu.CompilerParams(vmem_limit_bytes=VMEM_BYTES),
        cost_estimate=FREE,
        name="assemble",
    )(place, *map(in_hbm, pieces))
    return full.reshape(count * 2 * half, width)


def finish_kernel(jobs, owned, slots_ref, *refs):
    own_ref, refs = refs[0], refs[1:]
    count = sum(map(len, jobs))
    other_refs, (k_ref, down_ref, across_ref) = list(refs[:count]), refs[count:count + 3]
    out_ref, token_ref, mixed_ref = refs[-3:]
    step = pl.program_id(0)
    token_ref[...] = jnp.zeros_like(token_ref)
    for job, lengths in enumerate(jobs):
        parts = [(other_refs.pop(0), length) for length in lengths]

        @pl.when(step == job)
        def _(parts=parts):
            first = 0
            for other_ref, length in parts:
                rows = pl.ds(first, length)
                own = own_ref[0, rows]
                mixed_ref[rows] = (own + own) - other_ref[0]
                first += length

    cycle = jnp.dot(mixed_ref[...], k_ref[...], preferred_element_type=jnp.float32)
    denom = down_ref[0, :, 0:1] + across_ref[0, 0:1, :]
    kept = down_ref[0, :, 1:2] * across_ref[0, 1:2, :]
    out_ref[0] = (cycle * (kept / denom)).astype(out_ref.dtype)


def finish(first, first_row, jobs, slots, amps, integrals, down, across, so_far, own=None):
    _, _, width = amps.shape
    rows = sum(length for _, _, length in jobs[0])
    r = first_row // rows
    others = [other for job in jobs for other, _, _ in job]
    in_specs = [pl.BlockSpec((1, rows, width), lambda n, s: (s[first + n], r, 0)) if own is None else WHOLE]
    for job in jobs:
        for _, start, length in job:
            in_specs.append(pl.BlockSpec((1, length, width), lambda n, s, at=start // length: (0, at, 0)))
    in_specs += [
        WHOLE,
        pl.BlockSpec((1, rows, 2), lambda n, s: (s[first + n], r, 0)),
        pl.BlockSpec((1, 2, width), lambda n, s: (s[first + n], 0, 0)),
    ]
    operands = [slots, in_hbm(amps) if own is None else in_vmem(own)]
    operands += others + [in_vmem(integrals), down, across]
    aliases = {}
    if so_far is not None:
        aliases = {len(operands): 0}
        in_specs.append(ANY)
        operands.append(so_far)
    return pl.pallas_call(
        functools.partial(finish_kernel, [[length for _, _, length in job] for job in jobs], own is not None),
        grid_spec=pltpu.PrefetchScalarGridSpec(
            num_scalar_prefetch=1,
            grid=(len(jobs),),
            in_specs=in_specs,
            out_specs=[
                pl.BlockSpec((1, rows, width), lambda n, s: (s[first + n], r, 0)),
                pl.BlockSpec((8, 128), lambda n, s: (0, 0)),
            ],
            scratch_shapes=[pltpu.VMEM((rows, width), jnp.bfloat16)],
        ),
        out_shape=[jax.ShapeDtypeStruct(amps.shape, amps.dtype), jax.ShapeDtypeStruct((8, 128), jnp.float32)],
        input_output_aliases=aliases,
        compiler_params=pltpu.CompilerParams(vmem_limit_bytes=VMEM_BYTES),
        cost_estimate=FREE,
        name="finish",
    )(*operands)


def finish_together_kernel(first, first_row, jobs, columns, slots_ref, *refs):
    count = len(jobs)
    rows = sum(length for _, length in jobs[0])
    own_refs, refs = refs[:count], refs[count:]
    parts = sum(map(len, jobs))
    other_refs, (k_ref, down_ref, across_ref) = list(refs[:parts]), refs[parts:parts + 3]
    out_ref, mixed_ref, done_ref, sems = refs[-4:]
    for job, lengths in enumerate(jobs):
        at = 0
        for start, length in lengths:
            other_ref = other_refs.pop(0)
            own = own_refs[job][0, pl.ds(at, length)]
            mixed_ref[pl.ds(job * rows + at, length)] = (own + own) - other_ref[0, pl.ds(start, length)]
            at += length
    copies = []
    for n in range(out_ref.shape[2] // columns):
        part = pl.ds(n * columns, columns)
        cycle = jnp.dot(mixed_ref[...], k_ref[:, part], preferred_element_type=jnp.float32)
        for job in range(count):
            slot = slots_ref[first + job]
            mine, here = pl.ds(job * rows, rows), pl.ds(first_row, rows)
            denom = down_ref[slot, here, 0:1] + across_ref[slot, 0:1, part]
            kept = down_ref[slot, here, 1:2] * across_ref[slot, 1:2, part]
            done_ref[mine, part] = (cycle[job * rows:(job + 1) * rows] * (kept / denom)).astype(done_ref.dtype)
            target = out_ref.at[slot, here, part]
            copies.append(pltpu.make_async_copy(done_ref.at[mine, part], target, sems.at[len(copies)]))
            copies[-1].start()
    for copy in copies:
        copy.wait()


def finish_together(first, first_row, jobs, slots, owns, integrals, down, across, so_far, columns=512):
    width = integrals.shape[1]
    rows = sum(length for _, _, length in jobs[0])
    others = [other for job in jobs for other, _, _ in job]
    steps = width // columns
    operands = [slots, *map(in_vmem, owns), *others, in_vmem(integrals), down, across, so_far]
    return pl.pallas_call(
        functools.partial(
            finish_together_kernel, first, first_row, [[part[1:] for part in job] for job in jobs], columns
        ),
        in_specs=[SMEM] + [WHOLE] * (len(operands) - 2) + [ANY],
        out_specs=ANY,
        out_shape=jax.ShapeDtypeStruct(so_far.shape, so_far.dtype),
        scratch_shapes=[
            pltpu.VMEM((len(jobs) * rows, width), jnp.bfloat16),
            pltpu.VMEM((len(jobs) * rows, width), jnp.bfloat16),
            pltpu.SemaphoreType.DMA((steps * len(jobs),)),
        ],
        input_output_aliases={len(operands) - 1: 0},
        compiler_params=pltpu.CompilerParams(vmem_limit_bytes=VMEM_BYTES),
        cost_estimate=FREE,
        name="finish_together",
    )(*operands)


def local(amps, cycle_integrals, mirror, pair_list, tile_mask, occ_energy, virt_energy):
    pair_dev, rows, width = amps.shape
    devices, planes = lax.axis_size("pair"), lax.axis_size("virt")
    here, column = lax.axis_index("pair"), lax.axis_index("virt")
    stride = devices // pair_dev
    crossing = stride == 1 and pair_dev == 8 and planes == 4
    order = [0, 1, 6, 7, 2, 4, 3, 5] if crossing else list(range(pair_dev))
    core = here % 2

    def move(block, axis, to):
        n = lax.axis_size(axis)
        return lax.ppermute(block, axis, [(i, to(i)) for i in range(n)])

    if crossing:
        source = here ^ jnp.array(order, dtype=jnp.int32)
    else:
        source = (here + 1 + stride * jnp.arange(pair_dev, dtype=jnp.int32)) % devices
    entries = lax.dynamic_slice_in_dim(mirror, here * pair_dev, pair_dev, 0)
    slot = jnp.arange(pair_dev, dtype=jnp.int32)
    slots = jnp.sum(jnp.where(entries[None, :] // pair_dev == source[:, None], slot[None, :], 0), axis=1)

    def swap_cores(block):
        return move(block, "pair", lambda i: i ^ 1)

    lanes = jnp.repeat(tile_mask, TILE, axis=1).astype(jnp.float32)
    lanes_rows = lax.dynamic_slice_in_dim(lanes, column * rows, rows, 1)
    energy_rows = lax.dynamic_slice_in_dim(virt_energy, column * rows, rows, 0)
    orbitals = jnp.arange(occ_energy.shape[0], dtype=jnp.int32)
    first = jnp.sum(jnp.where(pair_list[:, 0:1] == orbitals[None, :], occ_energy[None, :], 0.0), axis=1)
    second = jnp.sum(jnp.where(pair_list[:, 1:2] == orbitals[None, :], occ_energy[None, :], 0.0), axis=1)
    occupied = first + second
    down = jnp.stack([energy_rows[None, :] - occupied[:, None], lanes_rows], axis=-1)
    across = jnp.stack([jnp.broadcast_to(virt_energy[None, :], lanes.shape), lanes], axis=1)

    def run(first, first_row, jobs, integrals, so_far):
        return finish(first, first_row, jobs, slots, amps, integrals, down, across, so_far)

    core_rows = cycle_integrals.shape[0] // 2
    place = jnp.stack([column, core]).astype(jnp.int32)
    if crossing:
        in_at = {step: at for at, step in enumerate(order)}
        quarter = rows // 4

        def peer(step):
            return lambda i: i ^ step

        def take(parts, earlier=(), outgoing=True, core_rows=0, staged=False):
            picks = [([(peer(step), first, count) for step, first, count in part], outgoing) for part in parts]
            return pick(picks, mirror, amps, cycle_integrals, core_rows, earlier, staged)

        def shift(value, step):
            return move(value, "pair", peer(step))

        def whole(step):
            return (step, 0, rows)

        def quarters(step, first, count):
            return (step, first * quarter, count * quarter)

        to_d, = take([[whole(6), whole(7)]], staged=True)
        to1, rows0 = take([[whole(1)]], [to_d], core_rows=core_rows, staged=True)
        from_d, from1 = shift(to_d, 6), swap_cores(to1)
        rows1, rows2 = move(rows0, "virt", lambda z: z ^ 1), move(rows0, "virt", lambda z: z ^ 2)
        rows3 = move(rows2, "virt", lambda z: z ^ 1)
        pieces = [rows0, rows1, rows2, rows3]
        pieces += [swap_cores(piece) for piece in pieces]
        integrals = assemble(pieces, [0, 1, 2, 3] * 2, [1] * 4 + [0] * 4, place, planes)
        to_x, to_y = take(
            [[whole(2), quarters(3, 0, 1)], [whole(4), quarters(5, 0, 1)]], [rows1, rows2, slots, down, across], staged=True
        )
        from_x, from_y = shift(to_x, 2), shift(to_y, 4)
        to0, = take([[whole(0)]], [rows1])
        tails = take([[quarters(3, 1, 2)], [quarters(5, 1, 2)]], [from_d])
        from3, from5 = shift(tails[0], 3), shift(tails[1], 5)
        swap_d = swap_cores(extract([(from_d, rows, rows)]))
        parts = [[(part, 0, rows)] for part in (to0, from1, from_d, swap_d)]
        result, done = run(0, 0, parts, integrals, None)
        last = take([[quarters(3, 3, 1)], [quarters(5, 3, 1)]], [from_d])
        owns = take([[whole(2)], [whole(4)]], [from_d], False)
        owns += take([[quarters(s, *q)] for q in ((0, 3), (3, 1)) for s in (3, 5)], [from_d], False)
        swapped = swap_cores(extract([(from_x, rows, quarter), (from_y, rows, quarter)], [done, *last, *owns]))
        last3, last5 = shift(last[0], 3), shift(last[1], 5)

        def together(first, first_row, parts, owns, so_far):
            return finish_together(first, first_row, parts, slots, owns, integrals, down, across, so_far)

        parts = [[(from_x, 0, rows)], [(from_y, 0, rows)]]
        result = together(in_at[2], 0, parts, owns[:2], result)
        parts = [[(swapped, n * quarter, quarter), (direct, 0, 2 * quarter)] for n, direct in enumerate((from3, from5))]
        result = together(in_at[3], 0, parts, owns[2:4], result)
        parts = [[(last3, 0, quarter)], [(last5, 0, quarter)]]
        result = together(in_at[3], 3 * quarter, parts, owns[4:], result)
    else:
        picks = []
        for k in range(pair_dev):
            offset = (1 + k * stride) % devices
            picks.append(([(lambda i, o=offset: lax.rem(i + devices - o, jnp.int32(devices)), 0, rows)], True))
        *to_all, rows0 = pick(picks, mirror, amps, cycle_integrals, core_rows)
        mine = [rows0] + [move(rows0, "virt", lambda z, s=s: (z - s) % planes) for s in range(1, planes)]
        other = [swap_cores(piece) for piece in mine]
        integrals = assemble(
            mine + other, 2 * list(range(planes)), [1] * planes + [0] * planes, place, planes
        )
        result = None
        for k in range(pair_dev):
            arrived = move(to_all[k], "pair", lambda i, k=k: (i - 1 - k * stride) % devices)
            result, _ = run(k, 0, [[(arrived, 0, rows)]], integrals, result)
    return result


def solution(mesh):
    return jax.shard_map(
        local,
        mesh=mesh,
        in_specs=(
            P("pair", "virt", None),
            P("virt", None),
            P(),
            P("pair", None),
            P("pair", None),
            P(),
            P(),
        ),
        out_specs=P("pair", "virt", None),
        check_vma=False,
    )
```
